32 devices in a mesh: ctx: 16 (over z, y, x), head: 2 (over core).
Axes of the slice: x: 2, y: 2, z: 4, core: 2. Of those that a mesh axis runs over, the one named last changes fastest.
Arguments:
- query_rows: float32 [4096, 4096], P('ctx', 'head'), may hold values from -6 to 6
- key_rows: float32 [2, 4096, 4096], P(None, 'ctx', 'head'), may hold values from -8 to 8
- reflection_value_rows: float32 [2, 4096, 4096], P(None, 'ctx', 'head'), may hold values from -6 to 6
- beta_logit: float32 [2, 32, 4096], P(None, 'head', 'ctx'), may hold values from -8 to 8
Outputs:
- normed: float32 [4096, 4096], P('ctx', 'head')
The draws below stay inside these ranges and needn't reach their ends.
All inputs are finite; a program needn't handle non-finite values.
Results may differ from the reference program's by a relative error of at most 0.00013.
Values sent between devices are 32-bit elements; how exact they have to be, the bound alone decides.
A program may use at most 128 MiB of HBM per device.

```python
import jax
import jax.numpy as jnp
from jax import lax

HEADS = 32
DK = 128
DV = 128
GROUP = 64
TOK_DEV = 256
SEQUENCE_TOKENS = 4096


def draw_key_rows(key, part):
    key = jax.random.fold_in(key, 23)
    random_seed_values = jax.random.split(key, 3)
    sign_pattern = 2.0 * jax.random.randint(random_seed_values[0], (HEADS, DK), 0, 2).astype(jnp.float32) - 1.0
    strength = jax.random.uniform(random_seed_values[1], (2, SEQUENCE_TOKENS, HEADS, 1), jnp.float32, 0.6, 1.4)
    spread = jnp.clip(jax.random.normal(random_seed_values[2], (2, SEQUENCE_TOKENS, HEADS, DK), jnp.float32), -6.0, 6.0)
    raw_keys = strength * sign_pattern[None, None, :, :] + spread
    return jnp.clip(raw_keys, -8.0, 8.0).reshape(2, SEQUENCE_TOKENS, HEADS * DK)


def draw_beta_logit(key, part):
    key = jax.random.fold_in(key, 11)
    random_seed_values = jax.random.split(key, 6)
    slow_share = 50
    medium_logit = -2.0 + 0.2 * jax.random.normal(random_seed_values[1], (2, HEADS, SEQUENCE_TOKENS), jnp.float32)
    reach_low = 0.5
    reach_high = 2.0
    token_jitter = jnp.clip(0.25 * jax.random.normal(random_seed_values[5], (2, HEADS, SEQUENCE_TOKENS), jnp.float32), -0.5, 0.5)
    sluggish_head_set = jax.random.randint(random_seed_values[0], (HEADS,), 0, 100) < slow_share
    reach_draw = jax.random.uniform(random_seed_values[2], (HEADS,), jnp.float32, 0.0, 1.0)
    reach_factor = jnp.exp(jnp.log(reach_low) + reach_draw * (jnp.log(reach_high) - jnp.log(reach_low)))
    target_strength = reach_factor * (DK / SEQUENCE_TOKENS)
    base_logit = jnp.log(target_strength / (2.0 - target_strength))
    block_shift = jnp.repeat(jax.random.uniform(random_seed_values[3], (SEQUENCE_TOKENS // TOK_DEV,), jnp.float32, -0.35, 0.35), TOK_DEV)
    slow_logit = base_logit[None, :, None] + token_jitter + block_shift[None, None, :]
    spike_location = jax.random.randint(random_seed_values[4], (4,), 0, SEQUENCE_TOKENS)
    spike_flag = jnp.any(jnp.arange(SEQUENCE_TOKENS)[:, None] == spike_location[None, :], axis=1)
    merged_logit = jnp.where(sluggish_head_set[None, :, None], slow_logit, medium_logit)
    merged_logit = jnp.where(spike_flag[None, None, :] & sluggish_head_set[None, :, None], 0.0, merged_logit)
    return jnp.clip(merged_logit, -8.0, 8.0)


def levels(own_key, extent, shards, least, high):
    gain = 1.0
    for dim, parts in shards:
        heights = jax.random.uniform(jax.random.fold_in(jax.random.fold_in(own_key, 6), dim), (parts,), jnp.float32, least / len(shards), high / len(shards))
        gain = gain * jnp.repeat(jnp.exp(heights), extent[dim] // parts).reshape((-1,) + (1,) * (len(extent) - 1 - dim))
    return gain


def noise(own_key, extent, scale, reach, cuts=(), held_as=jnp.bfloat16):
    drawn = scale * jax.random.normal(own_key, extent, jnp.float32)
    if cuts:
        drawn = drawn * levels(own_key, extent, cuts, -0.22, 0.18)
    return jnp.clip(drawn, -reach, reach).astype(held_as)


def setup_inputs(seed: int = 0) -> dict:
    seeds = jax.random.split(jax.random.key(seed), 5)
    return {
        "query_rows": noise(seeds[0], (SEQUENCE_TOKENS, HEADS * DK), 1.0, 6.0, ((0, 16), (1, 2)), jnp.float32),
        "key_rows": draw_key_rows(jax.random.fold_in(seeds[4], 71), 0),
        "reflection_value_rows": noise(seeds[2], (2, SEQUENCE_TOKENS, HEADS * DV), 1.0, 6.0, ((1, 16), (2, 2)), jnp.float32),
        "beta_logit": draw_beta_logit(jax.random.fold_in(seeds[4], 71), 0),
    }


highest_mode = lax.Precision.HIGHEST

def matmul_hi(left, right):
    return jnp.einsum('...ij,...jk->...ik', left, right, precision=highest_mode)

def unit_rows(matrix):
    return matrix * lax.rsqrt(lax.optimization_barrier(jnp.sum(matrix * matrix, axis=-1, keepdims=True)) + 1e-06)

def group_terms(query_blk, key_blk, value_blk, gate_strength_slab):
    width_v = value_blk.shape[-1]
    width_k = key_blk.shape[-1]
    steps_n = key_blk.shape[-2]
    rows_n = query_blk.shape[-2]
    key_gram = jnp.einsum('...id,...jd->...ij', key_blk, key_blk, precision=highest_mode)
    row_index = lax.broadcasted_iota(jnp.int32, (steps_n, steps_n), 0)
    col_index = lax.broadcasted_iota(jnp.int32, (steps_n, steps_n), 1)
    strict = row_index > col_index
    unit_lower = jnp.eye(steps_n, dtype=jnp.float32) + jnp.where(strict, gate_strength_slab[..., :, None] * key_gram, 0.0)
    right_cols = gate_strength_slab[..., :, None] * jnp.concatenate([value_blk, key_blk], axis=-1)
    solved = jax.scipy.linalg.solve_triangular(unit_lower, right_cols, lower=True, unit_diagonal=True)
    fresh_values = solved[..., :width_v]
    wy_keys = solved[..., width_v:]
    transition = jnp.eye(width_k, dtype=jnp.float32) - jnp.einsum('...id,...ie->...de', key_blk, wy_keys, precision=highest_mode)
    pushed = jnp.einsum('...id,...ie->...de', key_blk, fresh_values, precision=highest_mode)
    scores = jnp.einsum('...td,...id->...ti', query_blk, key_blk, precision=highest_mode)
    token_index = lax.broadcasted_iota(jnp.int32, (rows_n, steps_n), 0)
    sub_index = lax.broadcasted_iota(jnp.int32, (rows_n, steps_n), 1)
    causal_visible = sub_index // 2 <= token_index
    masked = jnp.where(causal_visible, scores, 0.0)
    query_eff = query_blk - matmul_hi(masked, wy_keys)
    inner_portion = matmul_hi(masked, fresh_values)
    return (transition, pushed, query_eff, inner_portion)

def reference(query_rows, key_rows, reflection_value_rows, beta_logit):
    groups = SEQUENCE_TOKENS // GROUP
    query_all = unit_rows(query_rows.reshape(groups, GROUP, HEADS, DK)).transpose(0, 2, 1, 3)
    key_full_tensor = unit_rows(key_rows.reshape(2, groups, GROUP, HEADS, DK)).transpose(1, 3, 2, 0, 4).reshape(groups, HEADS, 2 * GROUP, DK)
    value_all = reflection_value_rows.reshape(2, groups, GROUP, HEADS, DV).transpose(1, 3, 2, 0, 4).reshape(groups, HEADS, 2 * GROUP, DV)
    beta_all = (2.0 * jax.nn.sigmoid(beta_logit)).reshape(2, HEADS, groups, GROUP).transpose(2, 1, 3, 0).reshape(groups, HEADS, 2 * GROUP)

    def advance(memory, group_in):
        transition, pushed, query_eff, inner_portion = group_terms(group_in[0], group_in[1], group_in[2], group_in[3])
        return (matmul_hi(transition, memory) + pushed, matmul_hi(query_eff, memory) + inner_portion)
    initial_memory_matrix = jnp.zeros((HEADS, DK, DV), jnp.float32)
    _, outputs = lax.scan(advance, initial_memory_matrix, (query_all, key_full_tensor, value_all, beta_all))
    head_out = outputs.transpose(0, 2, 1, 3).reshape(SEQUENCE_TOKENS, HEADS * DV)
    mean_square = lax.optimization_barrier(jnp.mean(head_out * head_out, axis=-1, keepdims=True))
    return head_out * lax.rsqrt(mean_square + 1e-05)
```

```python
import functools

import jax
import jax.numpy as jnp
from jax import lax
from jax.experimental import pallas as pl
from jax.experimental.pallas import tpu as pltpu
from jax.sharding import PartitionSpec as P

DK = 128
DV = 128
GROUP = 64
SUB = 2 * GROUP
F32 = jnp.float32
BF16 = jnp.bfloat16
MESH = pl.DeviceIdType.MESH
VMEM_LIMIT = 48 * 1024 * 1024


def split(x):
    high = x.astype(BF16)
    return high, (x - high.astype(F32)).astype(BF16)


def wide(x):
    return jnp.concatenate(split(x), axis=1)


def tall(x):
    row = jnp.concatenate(split(x), axis=1)
    return jnp.concatenate([row, row], axis=0)


def product(left, right):
    both = jnp.dot(left, right, preferred_element_type=F32)
    width = both.shape[1] // 2
    return both[:, :width] + both[:, width:]


def terms_kernel(q_ref, k_ref, v_ref, b_ref, trans_ref, state_ref, qeff_ref, inner_ref):
    tokens = q_ref.shape[0]
    groups = range(tokens // GROUP)
    row = lax.broadcasted_iota(jnp.int32, (SUB, SUB), 0)
    col = lax.broadcasted_iota(jnp.int32, (SUB, SUB), 1)
    row_order = 2 * (row % GROUP) + row // GROUP
    col_order = 2 * (col % GROUP) + col // GROUP
    strict = row_order > col_order
    differ = row_order ^ col_order
    eye = jnp.where(row == col, 1.0, 0.0).astype(F32)
    token = lax.broadcasted_iota(jnp.int32, (GROUP, SUB), 0)
    key_token = lax.broadcasted_iota(jnp.int32, (GROUP, SUB), 1) % GROUP
    visible = key_token <= token

    query, key_t, right, lower, masked, inverse = [], [], [], [], [], []
    for g in groups:
        rows = slice(g * GROUP, (g + 1) * GROUP)
        q = q_ref[rows, :]
        q = q * lax.rsqrt(jnp.sum(q * q, axis=-1, keepdims=True) + 1e-06)
        k = jnp.concatenate([k_ref[0, rows, :], k_ref[1, rows, :]], axis=0)
        k = k * lax.rsqrt(jnp.sum(k * k, axis=-1, keepdims=True) + 1e-06)
        v = jnp.concatenate([v_ref[0, rows, :], v_ref[1, rows, :]], axis=0)
        beta = jnp.concatenate([b_ref[0, rows, 0:1], b_ref[0, rows, 1:2]], axis=0)
        kb = k * beta
        kt = k.T
        both = product(wide(jnp.concatenate([kb, q], axis=0)), tall(kt))
        low = jnp.where(strict, both[:SUB], 0.0)
        query.append(q)
        key_t.append(kt)
        right.append(jnp.concatenate([v * beta, kb], axis=1))
        lower.append(low)
        masked.append(jnp.where(visible, both[SUB:], 0.0))
        inverse.append(eye - jnp.where(differ == 1, low, 0.0))

    level = 1
    while (1 << level) < SUB:
        pick = (differ >> level) == 1
        step = [
            product(wide(jnp.where(pick, lower[g], 0.0)), tall(inverse[g])) for g in groups
        ]
        inverse = [
            inverse[g] - product(wide(inverse[g]), tall(step[g])) for g in groups
        ]
        level += 1

    solved = [product(wide(inverse[g]), tall(right[g])) for g in groups]
    terms = [
        product(wide(jnp.concatenate([key_t[g], masked[g]], axis=0)), tall(solved[g]))
        for g in groups
    ]
    prefix = None
    for g in groups:
        rows = slice(g * GROUP, (g + 1) * GROUP)
        pushed, inner = terms[g][:SUB, :DV], terms[g][SUB:, :DV]
        trans, qeff = eye - terms[g][:SUB, DV:], query[g] - terms[g][SUB:, DV:]
        if prefix is not None:
            moved = product(wide(jnp.concatenate([trans, qeff], axis=0)), tall(prefix))
            pushed = pushed + moved[:SUB, DK:]
            inner = inner + moved[SUB:, DK:]
            trans, qeff = moved[:SUB, :DK], moved[SUB:, :DK]
        qeff_ref[0, rows, :] = wide(qeff)
        inner_ref[rows, :] = inner
        prefix = jnp.concatenate([trans, pushed], axis=1)
    trans_ref[0] = wide(trans)
    state_ref[0] = pushed


def chain_kernel(
    ctx_n, head_n, width, trans_ref, state_ref, qeff_ref, inner_ref, out_ref,
    arriving, leaving, mine, theirs, send_sem, recv_sem, sum_send, sum_recv,
):
    heads, tokens = qeff_ref.shape[:2]
    me = lax.axis_index("ctx")
    core = lax.axis_index("head")
    peers = [lax.rem(core + off, head_n) for off in range(1, head_n)]

    barrier = pltpu.get_barrier_semaphore()
    for peer in peers:
        pl.semaphore_signal(barrier, inc=1, device_id=(me, peer), device_id_type=MESH)

    @pl.when(me > 0)
    def _():
        pl.semaphore_signal(barrier, inc=1, device_id=(me - 1, core), device_id_type=MESH)

    @pl.when(me < ctx_n - 1)
    def _():
        pl.semaphore_signal(barrier, inc=1, device_id=(me + 1, core), device_id_type=MESH)

    @pl.when(me == 0)
    def _():
        arriving[...] = jnp.zeros_like(arriving)

    neighbours = jnp.minimum(me, 1) + jnp.minimum(ctx_n - 1 - me, 1)
    pl.semaphore_wait(barrier, neighbours + (head_n - 1))

    mine[...] = jnp.zeros_like(mine)

    def copy_of(h, target):
        return pltpu.make_async_remote_copy(
            src_ref=leaving.at[h],
            dst_ref=arriving.at[h],
            send_sem=send_sem.at[h],
            recv_sem=recv_sem.at[h],
            device_id=(target, core),
            device_id_type=MESH,
        )

    def one_head(h, carry):
        @pl.when(me > 0)
        def _():
            copy_of(h, me).wait_recv()

        state = tall(arriving[h])

        @pl.when(me < ctx_n - 1)
        def _():
            leaving[h] = product(trans_ref[h], state) + state_ref[h]
            copy_of(h, me + 1).start()

        columns = pl.ds(pl.multiple_of(h * DV, DV), DV)
        read = product(qeff_ref[h], state) + inner_ref[:, columns]
        out_ref[:, columns] = read
        mine[...] += read * read
        return carry

    lax.fori_loop(0, heads, one_head, 0)

    def sum_copy(off):
        return pltpu.make_async_remote_copy(
            src_ref=mine,
            dst_ref=theirs.at[off],
            send_sem=sum_send.at[off],
            recv_sem=sum_recv.at[off],
            device_id=(me, peers[off]),
            device_id_type=MESH,
        )

    for off in range(head_n - 1):
        sum_copy(off).start()
    for off in range(head_n - 1):
        sum_copy(off).wait()

    total = mine[...]
    for off in range(head_n - 1):
        total = total + theirs[off]
    scale = lax.rsqrt(jnp.sum(total, axis=-1, keepdims=True) / width + 1e-05)
    scale = jnp.broadcast_to(scale, (tokens, DV))

    def scale_head(h, carry):
        columns = pl.ds(pl.multiple_of(h * DV, DV), DV)
        out_ref[:, columns] = out_ref[:, columns] * scale
        return carry

    lax.fori_loop(0, heads, scale_head, 0)

    @pl.when(me < ctx_n - 1)
    def _():
        def finish(h, carry):
            copy_of(h, me + 1).wait_send()
            return carry

        lax.fori_loop(0, heads, finish, 0)


def local(query_rows, key_rows, reflection_value_rows, beta_logit):
    tokens = query_rows.shape[0]
    heads = query_rows.shape[1] // DK
    ctx_n = lax.axis_size("ctx")
    head_n = lax.axis_size("head")
    beta = (2.0 * jax.nn.sigmoid(beta_logit)).transpose(1, 2, 0)
    shape = jax.ShapeDtypeStruct
    rows_of = pl.BlockSpec((tokens, DK), lambda h: (0, h))
    pair_of = pl.BlockSpec((2, tokens, DK), lambda h: (0, 0, h))

    def head_of(*block):
        return pl.BlockSpec((1,) + block, lambda h: (h, 0, 0))

    trans, state, qeff, inner = pl.pallas_call(
        terms_kernel,
        grid=(heads,),
        in_specs=[rows_of, pair_of, pair_of, head_of(tokens, 2)],
        out_specs=[head_of(DK, 2 * DK), head_of(DK, DV), head_of(tokens, 2 * DK), rows_of],
        out_shape=[
            shape((heads, DK, 2 * DK), BF16),
            shape((heads, DK, DV), F32),
            shape((heads, tokens, 2 * DK), BF16),
            shape((tokens, heads * DV), F32),
        ],
        compiler_params=pltpu.CompilerParams(vmem_limit_bytes=VMEM_LIMIT),
        name="terms",
    )(query_rows, key_rows, reflection_value_rows, beta)

    whole = pl.BlockSpec(memory_space=pltpu.VMEM)
    width = float(head_n * heads * DV)
    return pl.pallas_call(
        functools.partial(chain_kernel, ctx_n, head_n, width),
        in_specs=[whole] * 4,
        out_specs=whole,
        out_shape=shape((tokens, heads * DV), F32),
        scratch_shapes=[
            pltpu.VMEM((heads, DK, DV), F32),
            pltpu.VMEM((heads, DK, DV), F32),
            pltpu.VMEM((tokens, DV), F32),
            pltpu.VMEM((max(head_n - 1, 1), tokens, DV), F32),
            pltpu.SemaphoreType.DMA((heads,)),
            pltpu.SemaphoreType.DMA((heads,)),
            pltpu.SemaphoreType.DMA((max(head_n - 1, 1),)),
            pltpu.SemaphoreType.DMA((max(head_n - 1, 1),)),
        ],
        compiler_params=pltpu.CompilerParams(
            collective_id=0, has_side_effects=True, vmem_limit_bytes=VMEM_LIMIT
        ),
        name="chain",
    )(trans, state, qeff, inner)


def solution(mesh):
    placed = (
        P("ctx", "head"),
        P(None, "ctx", "head"),
        P(None, "ctx", "head"),
        P(None, "head", "ctx"),
    )
    return jax.shard_map(
        local, mesh=mesh, in_specs=placed, out_specs=P("ctx", "head"), check_vma=False
    )
```

```python
import functools

import jax
import jax.numpy as jnp
from jax import lax
from jax.experimental import pallas as pl
from jax.experimental.pallas import tpu as pltpu
from jax.sharding import PartitionSpec as P

DK = 128
DV = 128
GROUP = 64
SUB = 2 * GROUP
F32 = jnp.float32
BF16 = jnp.bfloat16
MESH = pl.DeviceIdType.MESH
VMEM_LIMIT = 48 * 1024 * 1024
PARTS = 2
LAG = 2


def split(x):
    high = x.astype(BF16)
    return high, (x - high.astype(F32)).astype(BF16)


def wide(x):
    return jnp.concatenate(split(x), axis=1)


def tall(x):
    row = jnp.concatenate(split(x), axis=1)
    return jnp.concatenate([row, row], axis=0)


def product(left, right):
    both = jnp.dot(left, right, preferred_element_type=F32)
    width = both.shape[1] // 2
    return both[:, :width] + both[:, width:]


def head_terms(h, q_ref, k_ref, v_ref, b_ref, trans_ref, state_ref, qeff_ref, inner_ref):
    columns = pl.ds(pl.multiple_of(h * DK, DK), DK)
    tokens = q_ref.shape[0]
    groups = range(tokens // GROUP)
    row = lax.broadcasted_iota(jnp.int32, (SUB, SUB), 0)
    col = lax.broadcasted_iota(jnp.int32, (SUB, SUB), 1)
    row_order = 2 * (row % GROUP) + row // GROUP
    col_order = 2 * (col % GROUP) + col // GROUP
    strict = row_order > col_order
    differ = row_order ^ col_order
    eye = jnp.where(row == col, 1.0, 0.0).astype(F32)
    token = lax.broadcasted_iota(jnp.int32, (GROUP, SUB), 0)
    key_token = lax.broadcasted_iota(jnp.int32, (GROUP, SUB), 1) % GROUP
    visible = key_token <= token

    query, key_t, right, lower, masked, inverse = [], [], [], [], [], []
    for g in groups:
        rows = slice(g * GROUP, (g + 1) * GROUP)
        q = q_ref[rows, columns]
        q = q * lax.rsqrt(jnp.sum(q * q, axis=-1, keepdims=True) + 1e-06)
        k = jnp.concatenate([k_ref[0, rows, columns], k_ref[1, rows, columns]], axis=0)
        k = k * lax.rsqrt(jnp.sum(k * k, axis=-1, keepdims=True) + 1e-06)
        v = jnp.concatenate([v_ref[0, rows, columns], v_ref[1, rows, columns]], axis=0)
        beta = jnp.concatenate([b_ref[h, rows, 0:1], b_ref[h, rows, 1:2]], axis=0)
        kb = k * beta
        kt = k.T
        both = product(wide(jnp.concatenate([kb, q], axis=0)), tall(kt))
        low = jnp.where(strict, both[:SUB], 0.0)
        query.append(q)
        key_t.append(kt)
        right.append(jnp.concatenate([v * beta, kb], axis=1))
        lower.append(low)
        masked.append(jnp.where(visible, both[SUB:], 0.0))
        inverse.append(eye - jnp.where(differ == 1, low, 0.0))

    level = 1
    while (1 << level) < SUB:
        pick = (differ >> level) == 1
        step = [
            product(wide(jnp.where(pick, lower[g], 0.0)), tall(inverse[g])) for g in groups
        ]
        inverse = [
            inverse[g] - product(wide(inverse[g]), tall(step[g])) for g in groups
        ]
        level += 1

    solved = [product(wide(inverse[g]), tall(right[g])) for g in groups]
    terms = [
        product(wide(jnp.concatenate([key_t[g], masked[g]], axis=0)), tall(solved[g]))
        for g in groups
    ]
    prefix = None
    for g in groups:
        rows = slice(g * GROUP, (g + 1) * GROUP)
        pushed, inner = terms[g][:SUB, :DV], terms[g][SUB:, :DV]
        trans, qeff = eye - terms[g][:SUB, DV:], query[g] - terms[g][SUB:, DV:]
        if prefix is not None:
            moved = product(wide(jnp.concatenate([trans, qeff], axis=0)), tall(prefix))
            pushed = pushed + moved[:SUB, DK:]
            inner = inner + moved[SUB:, DK:]
            trans, qeff = moved[:SUB, :DK], moved[SUB:, :DK]
        qeff_ref[h, rows, :] = wide(qeff)
        inner_ref[rows, columns] = inner
        prefix = jnp.concatenate([trans, pushed], axis=1)
    trans_ref[h] = tall(trans.T)
    state_ref[h] = pushed.T


def mixer_kernel(
    ctx_n, head_n, width, q_ref, k_ref, v_ref, b_ref, out_ref,
    trans_ref, state_ref, qeff_ref, arriving, leaving, mine, theirs,
    send_sem, recv_sem, sum_send, sum_recv,
):
    heads, tokens = qeff_ref.shape[:2]
    me = lax.axis_index("ctx")
    core = lax.axis_index("head")
    peers = [lax.rem(core + off, head_n) for off in range(1, head_n)]

    barrier = pltpu.get_barrier_semaphore()
    for peer in peers:
        pl.semaphore_signal(barrier, inc=1, device_id=(me, peer), device_id_type=MESH)

    @pl.when(me > 0)
    def _():
        pl.semaphore_signal(barrier, inc=1, device_id=(me - 1, core), device_id_type=MESH)

    @pl.when(me < ctx_n - 1)
    def _():
        pl.semaphore_signal(barrier, inc=1, device_id=(me + 1, core), device_id_type=MESH)

    neighbours = jnp.minimum(me, 1) + jnp.minimum(ctx_n - 1 - me, 1)
    pl.semaphore_wait(barrier, neighbours + (head_n - 1))

    mine[...] = jnp.zeros_like(mine)
    part = DV // PARTS

    def copy_of(h, c, target):
        rows = pl.ds(c * part, part)
        return pltpu.make_async_remote_copy(
            src_ref=leaving.at[h, rows],
            dst_ref=arriving.at[h, rows],
            send_sem=send_sem.at[h, c],
            recv_sem=recv_sem.at[h, c],
            device_id=(target, core),
            device_id_type=MESH,
        )

    def relay_head(h):
        for c in range(PARTS):
            rows = pl.ds(c * part, part)

            @pl.when(me == 0)
            def _():
                leaving[h, rows] = state_ref[h, rows]

            @pl.when(me > 0)
            def _():
                copy_of(h, c, me).wait_recv()
                leaving[h, rows] = (
                    product(wide(arriving[h, rows]), trans_ref[h]) + state_ref[h, rows]
                )

            @pl.when(me < ctx_n - 1)
            def _():
                copy_of(h, c, me + 1).start()

        columns = pl.ds(pl.multiple_of(h * DV, DV), DV)

        @pl.when(me > 0)
        def _():
            out_ref[:, columns] += product(qeff_ref[h], tall(arriving[h].T))

        read = out_ref[:, columns]
        mine[...] += read * read

    lag = jnp.minimum(LAG * me, heads)

    def step(i, carry):
        @pl.when(i < heads)
        def _():
            head_terms(
                i, q_ref, k_ref, v_ref, b_ref, trans_ref, state_ref, qeff_ref, out_ref
            )

        @pl.when(i >= lag)
        def _():
            relay_head(i - lag)

        return carry

    lax.fori_loop(0, heads + lag, step, 0)

    def sum_copy(off):
        return pltpu.make_async_remote_copy(
            src_ref=mine,
            dst_ref=theirs.at[off],
            send_sem=sum_send.at[off],
            recv_sem=sum_recv.at[off],
            device_id=(me, peers[off]),
            device_id_type=MESH,
        )

    for off in range(head_n - 1):
        sum_copy(off).start()
    for off in range(head_n - 1):
        sum_copy(off).wait()

    total = mine[...]
    for off in range(head_n - 1):
        total = total + theirs[off]
    scale = lax.rsqrt(jnp.sum(total, axis=-1, keepdims=True) / width + 1e-05)
    scale = jnp.broadcast_to(scale, (tokens, DV))

    def scale_head(h, carry):
        columns = pl.ds(pl.multiple_of(h * DV, DV), DV)
        out_ref[:, columns] = out_ref[:, columns] * scale
        return carry

    lax.fori_loop(0, heads, scale_head, 0)

    @pl.when(me < ctx_n - 1)
    def _():
        def finish(h, carry):
            for c in range(PARTS):
                copy_of(h, c, me + 1).wait_send()
            return carry

        lax.fori_loop(0, heads, finish, 0)


def local(query_rows, key_rows, reflection_value_rows, beta_logit):
    tokens = query_rows.shape[0]
    heads = query_rows.shape[1] // DK
    ctx_n = lax.axis_size("ctx")
    head_n = lax.axis_size("head")
    beta = (2.0 * jax.nn.sigmoid(beta_logit)).transpose(1, 2, 0)
    shape = jax.ShapeDtypeStruct
    whole = pl.BlockSpec(memory_space=pltpu.VMEM)
    width = float(head_n * heads * DV)
    return pl.pallas_call(
        functools.partial(mixer_kernel, ctx_n, head_n, width),
        in_specs=[whole] * 4,
        out_specs=whole,
        out_shape=shape((tokens, heads * DV), F32),
        scratch_shapes=[
            pltpu.VMEM((heads, 2 * DK, 2 * DK), BF16),
            pltpu.VMEM((heads, DV, DK), F32),
            pltpu.VMEM((heads, tokens, 2 * DK), BF16),
            pltpu.VMEM((heads, DV, DK), F32),
            pltpu.VMEM((heads, DV, DK), F32),
            pltpu.VMEM((tokens, DV), F32),
            pltpu.VMEM((max(head_n - 1, 1), tokens, DV), F32),
            pltpu.SemaphoreType.DMA((heads, PARTS)),
            pltpu.SemaphoreType.DMA((heads, PARTS)),
            pltpu.SemaphoreType.DMA((max(head_n - 1, 1),)),
            pltpu.SemaphoreType.DMA((max(head_n - 1, 1),)),
        ],
        compiler_params=pltpu.CompilerParams(
            collective_id=0, has_side_effects=True, vmem_limit_bytes=VMEM_LIMIT
        ),
        name="mixer",
    )(query_rows, key_rows, reflection_value_rows, beta)


def solution(mesh):
    placed = (
        P("ctx", "head"),
        P(None, "ctx", "head"),
        P(None, "ctx", "head"),
        P(None, "head", "ctx"),
    )
    return jax.shard_map(
        local, mesh=mesh, in_specs=placed, out_specs=P("ctx", "head"), check_vma=False
    )
```

```python
import functools

import jax
import jax.numpy as jnp
from jax import lax
from jax.experimental import pallas as pl
from jax.experimental.pallas import tpu as pltpu
from jax.sharding import PartitionSpec as P

DK = 128
DV = 128
GROUP = 64
SUB = 2 * GROUP
F32 = jnp.float32
BF16 = jnp.bfloat16
MESH = pl.DeviceIdType.MESH
VMEM_LIMIT = 48 * 1024 * 1024
PARTS = 2
TEAM = 4


def split(x):
    high = x.astype(BF16)
    return high, (x - high.astype(F32)).astype(BF16)


def wide(x):
    return jnp.concatenate(split(x), axis=1)


def tall(x):
    row = jnp.concatenate(split(x), axis=1)
    return jnp.concatenate([row, row], axis=0)


def product(left, right):
    both = jnp.dot(left, right, preferred_element_type=F32)
    width = both.shape[1] // 2
    return both[:, :width] + both[:, width:]


def head_terms(h, q_ref, k_ref, v_ref, b_ref, trans_ref, own_ref, qeff_ref, inner_ref):
    columns = pl.ds(pl.multiple_of(h * DK, DK), DK)
    tokens = q_ref.shape[0]
    groups = range(tokens // GROUP)
    row = lax.broadcasted_iota(jnp.int32, (SUB, SUB), 0)
    col = lax.broadcasted_iota(jnp.int32, (SUB, SUB), 1)
    row_order = 2 * (row % GROUP) + row // GROUP
    col_order = 2 * (col % GROUP) + col // GROUP
    strict = row_order > col_order
    differ = row_order ^ col_order
    eye = jnp.where(row == col, 1.0, 0.0).astype(F32)
    token = lax.broadcasted_iota(jnp.int32, (GROUP, SUB), 0)
    key_token = lax.broadcasted_iota(jnp.int32, (GROUP, SUB), 1) % GROUP
    visible = key_token <= token

    query, key_t, right, lower, masked, inverse = [], [], [], [], [], []
    for g in groups:
        rows = slice(g * GROUP, (g + 1) * GROUP)
        q = q_ref[rows, columns]
        q = q * lax.rsqrt(jnp.sum(q * q, axis=-1, keepdims=True) + 1e-06)
        k = jnp.concatenate([k_ref[0, rows, columns], k_ref[1, rows, columns]], axis=0)
        k = k * lax.rsqrt(jnp.sum(k * k, axis=-1, keepdims=True) + 1e-06)
        v = jnp.concatenate([v_ref[0, rows, columns], v_ref[1, rows, columns]], axis=0)
        beta = jnp.concatenate([b_ref[h, rows, 0:1], b_ref[h, rows, 1:2]], axis=0)
        kb = k * beta
        kt = k.T
        both = product(wide(jnp.concatenate([kb, q], axis=0)), tall(kt))
        low = jnp.where(strict, both[:SUB], 0.0)
        query.append(q)
        key_t.append(kt)
        right.append(jnp.concatenate([v * beta, kb], axis=1))
        lower.append(low)
        masked.append(jnp.where(visible, both[SUB:], 0.0))
        inverse.append(eye - jnp.where(differ == 1, low, 0.0))

    level = 1
    while (1 << level) < SUB:
        pick = (differ >> level) == 1
        step = [
            product(wide(jnp.where(pick, lower[g], 0.0)), tall(inverse[g])) for g in groups
        ]
        inverse = [
            inverse[g] - product(wide(inverse[g]), tall(step[g])) for g in groups
        ]
        level += 1

    solved = [product(wide(inverse[g]), tall(right[g])) for g in groups]
    terms = [
        product(wide(jnp.concatenate([key_t[g], masked[g]], axis=0)), tall(solved[g]))
        for g in groups
    ]
    prefix = None
    for g in groups:
        rows = slice(g * GROUP, (g + 1) * GROUP)
        pushed, inner = terms[g][:SUB, :DV], terms[g][SUB:, :DV]
        trans, qeff = eye - terms[g][:SUB, DV:], query[g] - terms[g][SUB:, DV:]
        if prefix is not None:
            moved = product(wide(jnp.concatenate([trans, qeff], axis=0)), tall(prefix))
            pushed = pushed + moved[:SUB, DK:]
            inner = inner + moved[SUB:, DK:]
            trans, qeff = moved[:SUB, :DK], moved[SUB:, :DK]
        qeff_ref[h, rows, :] = wide(qeff)
        inner_ref[rows, columns] = inner
        prefix = jnp.concatenate([trans, pushed], axis=1)
    trans_t = trans.T
    trans_ref[h] = tall(trans_t)
    own_ref[h] = jnp.concatenate([trans_t, pushed.T], axis=0)


def mixer_kernel(
    ctx_n, head_n, width, q_ref, k_ref, v_ref, b_ref, out_ref,
    trans_ref, own_ref, qeff_ref, before, after, state_in, state_out, mine, theirs,
    pair_send, pair_recv, state_send, state_recv, spread_send, sum_send, sum_recv,
):
    heads, tokens = qeff_ref.shape[:2]
    me = lax.axis_index("ctx")
    core = lax.axis_index("head")
    peers = [lax.rem(core + off, head_n) for off in range(1, head_n)]
    inner_n = TEAM if ctx_n % TEAM == 0 else 1
    outer_n = ctx_n // inner_n
    last = inner_n - 1
    team, rank = me // inner_n, lax.rem(me, inner_n)
    mates = [team * inner_n + lax.rem(rank + off, inner_n) for off in range(1, inner_n)]

    barrier = pltpu.get_barrier_semaphore()

    def greet(ctx, head):
        pl.semaphore_signal(barrier, inc=1, device_id=(ctx, head), device_id_type=MESH)

    for peer in peers:
        greet(me, peer)
    for mate in mates:
        greet(mate, core)

    @pl.when((rank == last) & (team > 0))
    def _():
        greet(me - inner_n, core)

    @pl.when((rank == last) & (team < outer_n - 1))
    def _():
        greet(me + inner_n, core)

    is_last = 1 - jnp.minimum(last - rank, 1)
    beyond = jnp.minimum(team, 1) + jnp.minimum(outer_n - 1 - team, 1)
    pl.semaphore_wait(barrier, is_last * beyond + (head_n - 1 + inner_n - 1))

    mine[...] = jnp.zeros_like(mine)
    part = DV // PARTS

    def pair_copy(h, c):
        rows = pl.ds(c * DK, DK)
        return pltpu.make_async_remote_copy(
            src_ref=after.at[h, rows],
            dst_ref=before.at[h, rows],
            send_sem=pair_send.at[h, c],
            recv_sem=pair_recv.at[h, c],
            device_id=(me + 1, core),
            device_id_type=MESH,
        )

    def state_copy(h, c):
        rows = pl.ds(c * part, part)
        return pltpu.make_async_remote_copy(
            src_ref=state_out.at[h, rows],
            dst_ref=state_in.at[h, rows],
            send_sem=state_send.at[h, c],
            recv_sem=state_recv.at[h, c],
            device_id=(me + inner_n, core),
            device_id_type=MESH,
        )

    def spread_copy(h, c, mate):
        rows = pl.ds(c * part, part)
        return pltpu.make_async_remote_copy(
            src_ref=state_in.at[h, rows],
            dst_ref=state_in.at[h, rows],
            send_sem=spread_send.at[h, c, mate],
            recv_sem=state_recv.at[h, c],
            device_id=(mates[mate], core),
            device_id_type=MESH,
        )

    def compose_head(h):
        for c in range(2):
            rows = pl.ds(c * DK, DK)

            @pl.when(rank == 0)
            def _():
                after[h, rows] = own_ref[h, rows]

            @pl.when(rank > 0)
            def _():
                pair_copy(h, c).wait_recv()
                moved = product(wide(before[h, rows]), trans_ref[h])
                after[h, rows] = moved if c == 0 else moved + own_ref[h, rows]

            @pl.when(rank < last)
            def _():
                pair_copy(h, c).start()

    def relay_head(h):
        for c in range(PARTS):
            rows = pl.ds(c * part, part)
            shifted = pl.ds(DK + c * part, part)

            @pl.when(team > 0)
            def _():
                state_copy(h, c).wait_recv()

            @pl.when((team > 0) & (team < outer_n - 1))
            def _():
                state_out[h, rows] = (
                    product(wide(state_in[h, rows]), tall(after[h, :DK])) + after[h, shifted]
                )

            @pl.when(team == 0)
            def _():
                state_out[h, rows] = after[h, shifted]

            @pl.when(team < outer_n - 1)
            def _():
                state_copy(h, c).start()

            @pl.when(team > 0)
            def _():
                for mate in range(inner_n - 1):
                    spread_copy(h, c, mate).start()

    def read_head(h):
        columns = pl.ds(pl.multiple_of(h * DV, DV), DV)

        @pl.when((rank < last) & (team > 0))
        def _():
            for c in range(PARTS):
                state_copy(h, c).wait_recv()

        @pl.when((rank == 0) & (team > 0))
        def _():
            out_ref[:, columns] += product(qeff_ref[h], tall(state_in[h].T))

        @pl.when((rank > 0) & (team == 0))
        def _():
            out_ref[:, columns] += product(qeff_ref[h], tall(before[h, DK:].T))

        @pl.when((rank > 0) & (team > 0))
        def _():
            state = product(wide(state_in[h]), tall(before[h, :DK])) + before[h, DK:]
            out_ref[:, columns] += product(qeff_ref[h], tall(state.T))

        read = out_ref[:, columns]
        mine[...] += read * read

    relay_lag = last + team
    read_lag = jnp.maximum(heads, relay_lag + 1)

    def step(i, carry):
        @pl.when(i < heads)
        def _():
            head_terms(i, q_ref, k_ref, v_ref, b_ref, trans_ref, own_ref, qeff_ref, out_ref)

        @pl.when((i >= rank) & (i < heads + rank))
        def _():
            compose_head(i - rank)

        @pl.when((rank == last) & (i >= relay_lag) & (i < heads + relay_lag))
        def _():
            relay_head(i - relay_lag)

        @pl.when(i >= read_lag)
        def _():
            read_head(i - read_lag)

        return carry

    lax.fori_loop(0, heads + read_lag, step, 0)

    def sum_copy(off):
        return pltpu.make_async_remote_copy(
            src_ref=mine,
            dst_ref=theirs.at[off],
            send_sem=sum_send.at[off],
            recv_sem=sum_recv.at[off],
            device_id=(me, peers[off]),
            device_id_type=MESH,
        )

    for off in range(head_n - 1):
        sum_copy(off).start()
    for off in range(head_n - 1):
        sum_copy(off).wait()

    total = mine[...]
    for off in range(head_n - 1):
        total = total + theirs[off]
    scale = lax.rsqrt(jnp.sum(total, axis=-1, keepdims=True) / width + 1e-05)
    scale = jnp.broadcast_to(scale, (tokens, DV))

    def scale_head(h, carry):
        columns = pl.ds(pl.multiple_of(h * DV, DV), DV)
        out_ref[:, columns] = out_ref[:, columns] * scale
        return carry

    lax.fori_loop(0, heads, scale_head, 0)

    def finish(h, carry):
        @pl.when(rank < last)
        def _():
            for c in range(2):
                pair_copy(h, c).wait_send()

        @pl.when((rank == last) & (team < outer_n - 1))
        def _():
            for c in range(PARTS):
                state_copy(h, c).wait_send()

        @pl.when((rank == last) & (team > 0))
        def _():
            for c in range(PARTS):
                for mate in range(inner_n - 1):
                    spread_copy(h, c, mate).wait_send()

        return carry

    lax.fori_loop(0, heads, finish, 0)


def local(query_rows, key_rows, reflection_value_rows, beta_logit):
    tokens = query_rows.shape[0]
    heads = query_rows.shape[1] // DK
    ctx_n = lax.axis_size("ctx")
    head_n = lax.axis_size("head")
    beta = (2.0 * jax.nn.sigmoid(beta_logit)).transpose(1, 2, 0)
    shape = jax.ShapeDtypeStruct
    whole = pl.BlockSpec(memory_space=pltpu.VMEM)
    width = float(head_n * heads * DV)
    return pl.pallas_call(
        functools.partial(mixer_kernel, ctx_n, head_n, width),
        in_specs=[whole] * 4,
        out_specs=whole,
        out_shape=shape((tokens, heads * DV), F32),
        scratch_shapes=[
            pltpu.VMEM((heads, 2 * DK, 2 * DK), BF16),
            pltpu.VMEM((heads, DK + DV, DK), F32),
            pltpu.VMEM((heads, tokens, 2 * DK), BF16),
            pltpu.VMEM((heads, DK + DV, DK), F32),
            pltpu.VMEM((heads, DK + DV, DK), F32),
            pltpu.VMEM((heads, DV, DK), F32),
            pltpu.VMEM((heads, DV, DK), F32),
            pltpu.VMEM((tokens, DV), F32),
            pltpu.VMEM((max(head_n - 1, 1), tokens, DV), F32),
            pltpu.SemaphoreType.DMA((heads, 2)),
            pltpu.SemaphoreType.DMA((heads, 2)),
            pltpu.SemaphoreType.DMA((heads, PARTS)),
            pltpu.SemaphoreType.DMA((heads, PARTS)),
            pltpu.SemaphoreType.DMA((heads, PARTS, TEAM)),
            pltpu.SemaphoreType.DMA((max(head_n - 1, 1),)),
            pltpu.SemaphoreType.DMA((max(head_n - 1, 1),)),
        ],
        compiler_params=pltpu.CompilerParams(
            collective_id=0, has_side_effects=True, vmem_limit_bytes=VMEM_LIMIT
        ),
        name="mixer",
    )(query_rows, key_rows, reflection_value_rows, beta)


def solution(mesh):
    placed = (
        P("ctx", "head"),
        P(None, "ctx", "head"),
        P(None, "ctx", "head"),
        P(None, "head", "ctx"),
    )
    return jax.shard_map(
        local, mesh=mesh, in_specs=placed, out_specs=P("ctx", "head"), check_vma=False
    )
```

```python
import functools

import jax
import jax.numpy as jnp
from jax import lax
from jax.experimental import pallas as pl
from jax.experimental.pallas import tpu as pltpu
from jax.sharding import PartitionSpec as P

DK = 128
DV = 128
GROUP = 64
SUB = 2 * GROUP
F32 = jnp.float32
BF16 = jnp.bfloat16
MESH = pl.DeviceIdType.MESH
VMEM_LIMIT = 48 * 1024 * 1024
PARTS = 2
TEAM = 4


def split(x):
    high = x.astype(BF16)
    return high, (x - high.astype(F32)).astype(BF16)


def wide(x):
    return jnp.concatenate(split(x), axis=1)


def tall(x):
    row = jnp.concatenate(split(x), axis=1)
    return jnp.concatenate([row, row], axis=0)


def product(left, right):
    both = jnp.dot(left, right, preferred_element_type=F32)
    width = both.shape[1] // 2
    return both[:, :width] + both[:, width:]


def heads_terms(first, count, q_ref, k_ref, v_ref, b_ref, trans_ref, own_ref, qeff_ref, inner_ref):
    tokens = q_ref.shape[0]
    per_head = tokens // GROUP
    groups = range(count * per_head)
    row = lax.broadcasted_iota(jnp.int32, (SUB, SUB), 0)
    col = lax.broadcasted_iota(jnp.int32, (SUB, SUB), 1)
    row_order = 2 * (row % GROUP) + row // GROUP
    col_order = 2 * (col % GROUP) + col // GROUP
    strict = row_order > col_order
    differ = row_order ^ col_order
    eye = jnp.where(row == col, 1.0, 0.0).astype(F32)
    token = lax.broadcasted_iota(jnp.int32, (GROUP, SUB), 0)
    key_token = lax.broadcasted_iota(jnp.int32, (GROUP, SUB), 1) % GROUP
    visible = key_token <= token

    betas = jnp.concatenate(
        [jnp.broadcast_to(b_ref[j, pl.ds(first + u, 1), :], (8, tokens)) for u in range(count) for j in range(2)],
        axis=0,
    )
    betas = (2.0 / (1.0 + jnp.exp(-betas))).T

    query, key_t, right, lower, masked, inverse = [], [], [], [], [], []
    for g in groups:
        h = first + g // per_head
        columns = pl.ds(pl.multiple_of(h * DK, DK), DK)
        rows = slice(g % per_head * GROUP, (g % per_head + 1) * GROUP)
        q = q_ref[rows, columns]
        q = q * lax.rsqrt(jnp.sum(q * q, axis=-1, keepdims=True) + 1e-06)
        k = jnp.concatenate([k_ref[0, rows, columns], k_ref[1, rows, columns]], axis=0)
        k = k * lax.rsqrt(jnp.sum(k * k, axis=-1, keepdims=True) + 1e-06)
        v = jnp.concatenate([v_ref[0, rows, columns], v_ref[1, rows, columns]], axis=0)
        c = 16 * (g // per_head)
        beta = jnp.concatenate([betas[rows, c : c + 1], betas[rows, c + 8 : c + 9]], axis=0)
        kb = k * beta
        kt = k.T
        both = product(wide(jnp.concatenate([kb, q], axis=0)), tall(kt))
        low = jnp.where(strict, both[:SUB], 0.0)
        query.append(q)
        key_t.append(kt)
        right.append(jnp.concatenate([v * beta, kb], axis=1))
        lower.append(low)
        masked.append(jnp.where(visible, both[SUB:], 0.0))
        inverse.append(eye - jnp.where(differ == 1, low, 0.0))

    level = 1
    while (1 << level) < SUB:
        pick = (differ >> level) == 1
        step = [
            product(wide(jnp.where(pick, lower[g], 0.0)), tall(inverse[g])) for g in groups
        ]
        inverse = [
            inverse[g] - product(wide(inverse[g]), tall(step[g])) for g in groups
        ]
        level += 1

    solved = [product(wide(inverse[g]), tall(right[g])) for g in groups]
    terms = [
        product(wide(jnp.concatenate([key_t[g], masked[g]], axis=0)), tall(solved[g]))
        for g in groups
    ]
    prefix = None
    for g in groups:
        h = first + g // per_head
        columns = pl.ds(pl.multiple_of(h * DK, DK), DK)
        rows = slice(g % per_head * GROUP, (g % per_head + 1) * GROUP)
        pushed, inner = terms[g][:SUB, :DV], terms[g][SUB:, :DV]
        trans, qeff = eye - terms[g][:SUB, DV:], query[g] - terms[g][SUB:, DV:]
        if g % per_head:
            moved = product(wide(jnp.concatenate([trans, qeff], axis=0)), tall(prefix))
            pushed = pushed + moved[:SUB, DK:]
            inner = inner + moved[SUB:, DK:]
            trans, qeff = moved[:SUB, :DK], moved[SUB:, :DK]
        qeff_ref[h, rows, :] = wide(qeff)
        inner_ref[rows, columns] = inner
        prefix = jnp.concatenate([trans, pushed], axis=1)
        if g % per_head == per_head - 1:
            trans_t = trans.T
            trans_ref[h] = tall(trans_t)
            own_ref[h] = jnp.concatenate([trans_t, pushed.T], axis=0)


def mixer_kernel(
    ctx_n, head_n, width, q_ref, k_ref, v_ref, b_ref, out_ref,
    trans_ref, own_ref, qeff_ref, before, after, state_in, state_out, mine, theirs,
    pair_send, pair_recv, state_send, state_recv, spread_send, sum_send, sum_recv,
):
    heads, tokens = qeff_ref.shape[:2]
    me = lax.axis_index("ctx")
    core = lax.axis_index("head")
    peers = [lax.rem(core + off, head_n) for off in range(1, head_n)]
    inner_n = TEAM if ctx_n % TEAM == 0 else 1
    outer_n = ctx_n // inner_n
    last = inner_n - 1
    team, rank = me // inner_n, lax.rem(me, inner_n)
    mates = [team * inner_n + lax.rem(rank + off, inner_n) for off in range(1, inner_n)]

    barrier = pltpu.get_barrier_semaphore()

    def greet(ctx, head):
        pl.semaphore_signal(barrier, inc=1, device_id=(ctx, head), device_id_type=MESH)

    for peer in peers:
        greet(me, peer)
    for mate in mates:
        greet(mate, core)

    @pl.when((rank == last) & (team > 0))
    def _():
        greet(me - inner_n, core)

    @pl.when((rank == last) & (team < outer_n - 1))
    def _():
        greet(me + inner_n, core)

    is_last = 1 - jnp.minimum(last - rank, 1)
    beyond = jnp.minimum(team, 1) + jnp.minimum(outer_n - 1 - team, 1)
    pl.semaphore_wait(barrier, is_last * beyond + (head_n - 1 + inner_n - 1))

    mine[...] = jnp.zeros_like(mine)
    part = DV // PARTS

    def pair_copy(h, c):
        rows = pl.ds(c * DK, DK)
        return pltpu.make_async_remote_copy(
            src_ref=after.at[h, rows],
            dst_ref=before.at[h, rows],
            send_sem=pair_send.at[h, c],
            recv_sem=pair_recv.at[h, c],
            device_id=(me + 1, core),
            device_id_type=MESH,
        )

    def state_copy(h, c):
        rows = pl.ds(c * part, part)
        return pltpu.make_async_remote_copy(
            src_ref=state_out.at[h, rows],
            dst_ref=state_in.at[h, rows],
            send_sem=state_send.at[h, c],
            recv_sem=state_recv.at[h, c],
            device_id=(me + inner_n, core),
            device_id_type=MESH,
        )

    def spread_copy(h, c, mate):
        rows = pl.ds(c * part, part)
        return pltpu.make_async_remote_copy(
            src_ref=state_in.at[h, rows],
            dst_ref=state_in.at[h, rows],
            send_sem=spread_send.at[h, c, mate],
            recv_sem=state_recv.at[h, c],
            device_id=(mates[mate], core),
            device_id_type=MESH,
        )

    def compose_head(h):
        for c in range(2):
            rows = pl.ds(c * DK, DK)

            @pl.when(rank == 0)
            def _():
                after[h, rows] = own_ref[h, rows]

            @pl.when(rank > 0)
            def _():
                pair_copy(h, c).wait_recv()
                moved = product(wide(before[h, rows]), trans_ref[h])
                after[h, rows] = moved if c == 0 else moved + own_ref[h, rows]

            @pl.when(rank < last)
            def _():
                pair_copy(h, c).start()

    def relay_head(h):
        for c in range(PARTS):
            rows = pl.ds(c * part, part)
            shifted = pl.ds(DK + c * part, part)

            @pl.when(team > 0)
            def _():
                state_copy(h, c).wait_recv()

            @pl.when((team > 0) & (team < outer_n - 1))
            def _():
                state_out[h, rows] = (
                    product(wide(state_in[h, rows]), tall(after[h, :DK])) + after[h, shifted]
                )

            @pl.when(team == 0)
            def _():
                state_out[h, rows] = after[h, shifted]

            @pl.when(team < outer_n - 1)
            def _():
                state_copy(h, c).start()

            @pl.when(team > 0)
            def _():
                for mate in range(inner_n - 1):
                    spread_copy(h, c, mate).start()

    def read_head(h):
        columns = pl.ds(pl.multiple_of(h * DV, DV), DV)

        @pl.when((rank < last) & (team > 0))
        def _():
            for c in range(PARTS):
                state_copy(h, c).wait_recv()

        @pl.when((rank == 0) & (team > 0))
        def _():
            out_ref[:, columns] += product(qeff_ref[h], tall(state_in[h].T))

        @pl.when((rank > 0) & (team == 0))
        def _():
            out_ref[:, columns] += product(qeff_ref[h], tall(before[h, DK:].T))

        @pl.when((rank > 0) & (team > 0))
        def _():
            state = product(wide(state_in[h]), tall(before[h, :DK])) + before[h, DK:]
            out_ref[:, columns] += product(qeff_ref[h], tall(state.T))

        read = out_ref[:, columns]
        mine[...] += read * read

    relay_lag = last + team
    read_lag = jnp.maximum(heads, relay_lag + 1)

    at_once = 2 if heads % 2 == 0 else 1

    def step(i, carry):
        @pl.when((i < heads) & (lax.rem(i, at_once) == 0))
        def _():
            heads_terms(i, at_once, q_ref, k_ref, v_ref, b_ref, trans_ref, own_ref, qeff_ref, out_ref)

        @pl.when((i >= rank) & (i < heads + rank))
        def _():
            compose_head(i - rank)

        @pl.when((rank == last) & (i >= relay_lag) & (i < heads + relay_lag))
        def _():
            relay_head(i - relay_lag)

        @pl.when(i >= read_lag)
        def _():
            read_head(i - read_lag)

        return carry

    lax.fori_loop(0, heads + read_lag, step, 0)

    def sum_copy(off):
        return pltpu.make_async_remote_copy(
            src_ref=mine,
            dst_ref=theirs.at[off],
            send_sem=sum_send.at[off],
            recv_sem=sum_recv.at[off],
            device_id=(me, peers[off]),
            device_id_type=MESH,
        )

    for off in range(head_n - 1):
        sum_copy(off).start()
    for off in range(head_n - 1):
        sum_copy(off).wait()

    total = mine[...]
    for off in range(head_n - 1):
        total = total + theirs[off]
    scale = lax.rsqrt(jnp.sum(total, axis=-1, keepdims=True) / width + 1e-05)
    scale = jnp.broadcast_to(scale, (tokens, DV))

    def scale_head(h, carry):
        columns = pl.ds(pl.multiple_of(h * DV, DV), DV)
        out_ref[:, columns] = out_ref[:, columns] * scale
        return carry

    lax.fori_loop(0, heads, scale_head, 0)

    def finish(h, carry):
        @pl.when(rank < last)
        def _():
            for c in range(2):
                pair_copy(h, c).wait_send()

        @pl.when((rank == last) & (team < outer_n - 1))
        def _():
            for c in range(PARTS):
                state_copy(h, c).wait_send()

        @pl.when((rank == last) & (team > 0))
        def _():
            for c in range(PARTS):
                for mate in range(inner_n - 1):
                    spread_copy(h, c, mate).wait_send()

        return carry

    lax.fori_loop(0, heads, finish, 0)


def local(query_rows, key_rows, reflection_value_rows, beta_logit):
    tokens = query_rows.shape[0]
    heads = query_rows.shape[1] // DK
    ctx_n = lax.axis_size("ctx")
    head_n = lax.axis_size("head")
    shape = jax.ShapeDtypeStruct
    whole = pl.BlockSpec(memory_space=pltpu.VMEM)
    width = float(head_n * heads * DV)
    return pl.pallas_call(
        functools.partial(mixer_kernel, ctx_n, head_n, width),
        in_specs=[whole] * 4,
        out_specs=whole,
        out_shape=shape((tokens, heads * DV), F32),
        scratch_shapes=[
            pltpu.VMEM((heads, 2 * DK, 2 * DK), BF16),
            pltpu.VMEM((heads, DK + DV, DK), F32),
            pltpu.VMEM((heads, tokens, 2 * DK), BF16),
            pltpu.VMEM((heads, DK + DV, DK), F32),
            pltpu.VMEM((heads, DK + DV, DK), F32),
            pltpu.VMEM((heads, DV, DK), F32),
            pltpu.VMEM((heads, DV, DK), F32),
            pltpu.VMEM((tokens, DV), F32),
            pltpu.VMEM((max(head_n - 1, 1), tokens, DV), F32),
            pltpu.SemaphoreType.DMA((heads, 2)),
            pltpu.SemaphoreType.DMA((heads, 2)),
            pltpu.SemaphoreType.DMA((heads, PARTS)),
            pltpu.SemaphoreType.DMA((heads, PARTS)),
            pltpu.SemaphoreType.DMA((heads, PARTS, TEAM)),
            pltpu.SemaphoreType.DMA((max(head_n - 1, 1),)),
            pltpu.SemaphoreType.DMA((max(head_n - 1, 1),)),
        ],
        compiler_params=pltpu.CompilerParams(
            collective_id=0, has_side_effects=True, vmem_limit_bytes=VMEM_LIMIT
        ),
        name="mixer",
    )(query_rows, key_rows, reflection_value_rows, beta_logit)


def solution(mesh):
    placed = (
        P("ctx", "head"),
        P(None, "ctx", "head"),
        P(None, "ctx", "head"),
        P(None, "head", "ctx"),
    )
    return jax.shard_map(
        local, mesh=mesh, in_specs=placed, out_specs=P("ctx", "head"), check_vma=False
    )
```
